32 devices in a mesh: replica: 2 (over y), gx: 8 (over z, x), gy: 2 (over core).
Axes of the slice: x: 2, y: 2, z: 4, core: 2. Of those that a mesh axis runs over, the one named last changes fastest.
Arguments:
- tokens: bfloat16 [2, 128, 8192], P(None, ('replica', 'gy'), 'gx'), parts along dimension 1, may hold values from -6 to 6
- gate_weight: bfloat16 [8192, 26624], P('gx', 'gy'), may hold values from -0.09375 to 0.09375
- up_weight: bfloat16 [8192, 26624], P('gx', 'gy'), may hold values from -0.09375 to 0.09375
- down_weight: bfloat16 [26624, 8192], P('gy', 'gx'), may hold values from -0.0390625 to 0.0390625
Outputs:
- mixed: bfloat16 [2, 128, 8192], P(None, ('replica', 'gy'), 'gx'), parts along dimension 1
The draws below stay inside these ranges and needn't reach their ends.
There are 2 independent parts, one for each index of `replica`. The reference program is written for one: setup_inputs(seed, part) draws one part's arguments, and reference() takes and returns one part's arrays. A program takes and returns all parts, laid end to end along the dimension named above; an argument that names none is the same for every part. Nothing has to cross between parts.
All inputs are finite; a program needn't handle non-finite values.
Results may differ from the reference program's by a relative error of at most 0.015.
Values may be sent and summed in bfloat16 or wider, within the bound.
No kernel may reach another device: no remote copies, remote signals or barrier semaphores. Data moves between devices by JAX's collectives and lax.ppermute only.
A program may use at most 384 MiB of HBM per device.

```python
import jax
import jax.numpy as jnp

D = 8192
FF = 26624
BATCH = 64


def with_spikes(array, stream_key, source, target, shards_of, factor):
    def block_of(dim):
        return (jnp.arange(array.shape[dim]) // (array.shape[dim] // shards_of)).reshape((-1,) + (1,) * (array.ndim - 1 - dim))

    first = jax.random.permutation(stream_key, shards_of)[block_of(target)]
    far = (block_of(target) + shards_of // 2) % shards_of
    return jnp.where((block_of(source) == first) | (block_of(source) == far), factor * array, array)


def levels(rng, shape, pieces, low, largest):
    loudness = 1.0
    for position, parts in pieces:
        draws = jax.random.uniform(jax.random.fold_in(jax.random.fold_in(rng, 6), position), (parts,), jnp.float32, low / len(pieces), largest / len(pieces))
        loudness = loudness * jnp.repeat(jnp.exp(draws), shape[position] // parts).reshape((-1,) + (1,) * (len(shape) - 1 - position))
    return loudness


def normal_values(key, shape, width, most, shards=(), dtype=jnp.bfloat16):
    array = jax.random.normal(key, shape, jnp.float32) * width
    if len(shards) > 0:
        array = levels(key, shape, shards, -0.22, 0.18) * array
    return jnp.clip(array, min=-most, max=most).astype(dtype)


def gaussian_with(rng, extent, spread, reach, split, heavy, kind=jnp.bfloat16):
    values = spread * jax.random.normal(rng, extent, jnp.float32)
    if split:
        values = values * levels(rng, extent, split, -0.22, 0.18)
    return jnp.clip(with_spikes(values, jax.random.fold_in(rng, 3), *heavy), -reach, reach).astype(kind)


def setup_inputs(seed: int = 0, part: int = 0) -> dict:
    key_list = jax.random.split(jax.random.key(seed), 5)
    part_splits = jax.random.split(jax.random.fold_in(key_list[4], part), 5)
    return {
        "tokens": normal_values(part_splits[0], (2, BATCH, D), 1.0, 6.0, ((1, 2), (2, 8))),
        "gate_weight": gaussian_with(key_list[1], (D, FF), D ** -0.5, 0.09375, ((0, 8), (1, 2)), (0, 1, 8, 2.0)),
        "up_weight": gaussian_with(key_list[2], (D, FF), D ** -0.5, 0.09375, ((0, 8), (1, 2)), (0, 1, 8, 2.0)),
        "down_weight": normal_values(key_list[3], (FF, D), FF ** -0.5, 0.0390625, ((0, 2), (1, 8))),
    }


def layer_apply(inputs, gate_weight, up_weight, down_weight):
    gate = jnp.dot(inputs, gate_weight, preferred_element_type=jnp.float32)
    up = jnp.dot(inputs, up_weight, preferred_element_type=jnp.float32)
    hidden = (jax.nn.silu(gate) * up).astype(jnp.bfloat16)
    return jnp.dot(hidden, down_weight, preferred_element_type=jnp.float32).astype(jnp.bfloat16)


def reference(tokens, gate_weight, up_weight, down_weight):
    first_out = layer_apply(tokens[0], gate_weight, up_weight, down_weight)
    second_input = (tokens[1].astype(jnp.float32) + first_out.astype(jnp.float32)).astype(jnp.bfloat16)
    second_out = layer_apply(second_input, gate_weight, up_weight, down_weight)
    return jnp.stack([first_out, second_out])
```

```python
import jax
import jax.numpy as jnp
from jax import lax
from jax.experimental import pallas as pl
from jax.experimental.pallas import tpu as pltpu
from jax.sharding import PartitionSpec as P

BF16 = jnp.bfloat16
F32 = jnp.float32
BLOCK = 512
CHUNKS = ((4, 3), (3, 3))
STREAM_BITS = ((0, 1), (1, 0))
FAR = 2
VMEM = pl.BlockSpec(memory_space=pltpu.VMEM)
SMEM = pl.BlockSpec(memory_space=pltpu.SMEM)
HBM = pl.BlockSpec(memory_space=pltpu.HBM)
PARAMS = pltpu.CompilerParams(vmem_limit_bytes=24 * 2**20)


def swap(array, bit):
    return lax.ppermute(array, "gx", [(i, i ^ (1 << bit)) for i in range(8)])


def cost(flops, nbytes, exps=0):
    return pl.CostEstimate(flops=flops, bytes_accessed=nbytes, transcendentals=exps)


def aligned(index, step):
    return pl.ds(pl.multiple_of(index * step, 128), step)


def gate_up(v, gate_weight, up_weight, starts, counts, out_type):
    rows, depth = v.shape
    blocks = sum(counts)

    def kernel(starts_ref, v_ref, gate_ref, up_ref, *rest):
        out_refs, (held, sems) = rest[: len(counts)], rest[len(counts) :]
        firsts = [sum(counts[:r]) for r in range(len(counts))]

        def copy(r, i, which):
            columns = pl.ds(pl.multiple_of((starts_ref[r] + i) * BLOCK, BLOCK), BLOCK)
            slot = firsts[r] + i
            source = (gate_ref, up_ref)[which].at[:, columns]
            return pltpu.make_async_copy(source, held.at[slot, which], sems.at[slot, which])

        for r, n in enumerate(counts):
            for i in range(n):
                for which in range(2):
                    copy(r, i, which).start()
        for r, n in enumerate(counts):

            @pl.loop(0, n)
            def _(i):
                for which in range(2):
                    copy(r, i, which).wait()
                    out_refs[r][which, :, aligned(i, BLOCK)] = jnp.dot(
                        v_ref[...], held[firsts[r] + i, which], preferred_element_type=F32
                    ).astype(out_type)

    out = pl.pallas_call(
        kernel,
        out_shape=[jax.ShapeDtypeStruct((2, rows, n * BLOCK), out_type) for n in counts],
        in_specs=[SMEM, VMEM, HBM, HBM],
        out_specs=[VMEM] * len(counts),
        scratch_shapes=[
            pltpu.VMEM((blocks, 2, depth, BLOCK), BF16),
            pltpu.SemaphoreType.DMA((blocks, 2)),
        ],
        compiler_params=PARAMS,
        cost_estimate=cost(4 * rows * depth * blocks * BLOCK, 4 * depth * blocks * BLOCK),
        name="gate_up",
    )(jnp.stack(starts), v, gate_weight, up_weight)
    return list(out)


def down(total, hiddens, down_weight, starts):
    rows = hiddens[0].shape[0]
    columns = down_weight.shape[1]
    counts = [h.shape[1] // BLOCK for h in hiddens]
    blocks = sum(counts)

    def kernel(starts_ref, *rest):
        hidden_refs, rest = rest[: len(counts)], rest[len(counts) :]
        total_ref, rest = (rest[0], rest[1:]) if total is not None else (None, rest)
        weight_ref, out_ref, held, sems = rest
        firsts = [sum(counts[:r]) for r in range(len(counts))]

        def copy(r, i):
            at = pl.ds(pl.multiple_of((starts_ref[r] + i) * BLOCK, BLOCK), BLOCK)
            slot = firsts[r] + i
            return pltpu.make_async_copy(weight_ref.at[at, :], held.at[slot], sems.at[slot])

        for r, n in enumerate(counts):
            for i in range(n):
                copy(r, i).start()
        out_ref[...] = jnp.zeros_like(out_ref) if total_ref is None else total_ref[...]
        for r, n in enumerate(counts):

            @pl.loop(0, n)
            def _(i):
                copy(r, i).wait()
                out_ref[...] += jnp.dot(
                    hidden_refs[r][:, aligned(i, BLOCK)],
                    held[firsts[r] + i],
                    preferred_element_type=F32,
                )

    totals = [] if total is None else [total]
    return pl.pallas_call(
        kernel,
        out_shape=jax.ShapeDtypeStruct((rows, columns), F32),
        in_specs=[SMEM] + [VMEM] * (len(counts) + len(totals)) + [HBM],
        out_specs=VMEM,
        scratch_shapes=[
            pltpu.VMEM((blocks, BLOCK, columns), BF16),
            pltpu.SemaphoreType.DMA((blocks,)),
        ],
        compiler_params=PARAMS,
        cost_estimate=cost(2 * rows * columns * blocks * BLOCK, 2 * columns * blocks * BLOCK),
        name="down",
    )(jnp.stack(starts), *hiddens, *totals, down_weight)


def small(name, kernel, out_shape, *operands):
    n = sum(o.size for o in operands[1:])
    return pl.pallas_call(
        kernel,
        out_shape=out_shape,
        in_specs=[SMEM] + [VMEM] * (len(operands) - 1),
        out_specs=jax.tree.map(lambda _: VMEM, out_shape),
        compiler_params=PARAMS,
        cost_estimate=cost(2 * n, 8 * n),
        name=name,
    )(*operands)


def shape(dims, dtype):
    return jax.ShapeDtypeStruct(dims, dtype)


def halve(bits, bit, kept, received):
    _, rows, width = kept.shape
    half = width // 2

    def kernel(bits_ref, kept_ref, received_ref, own_ref, send_ref):
        mine, theirs = aligned(bits_ref[bit], half), aligned(1 - bits_ref[bit], half)
        send_ref[...] = (kept_ref[:, :, theirs] + received_ref[:, :, theirs].astype(F32)).astype(BF16)
        own_ref[...] = kept_ref[:, :, mine] + received_ref[:, :, mine].astype(F32)

    dims = (2, rows, half)
    return small("halve", kernel, [shape(dims, F32), shape(dims, BF16)], bits, kept, received)


def halve_far(bits, kepts, receiveds):
    rows = kepts[0].shape[1]
    halves = [k.shape[2] // 2 for k in kepts]

    def kernel(bits_ref, *refs):
        kept_refs, received_refs = refs[: len(halves)], refs[len(halves) : -2]
        own_ref, send_ref = refs[-2:]
        at = 0
        for kept_ref, received_ref, half in zip(kept_refs, received_refs, halves):
            to = slice(at, at + half)
            mine, theirs = aligned(bits_ref[FAR], half), aligned(1 - bits_ref[FAR], half)
            send_ref[:, :, to] = (
                kept_ref[:, :, theirs] + received_ref[:, :, theirs].astype(F32)
            ).astype(BF16)
            own_ref[:, :, to] = kept_ref[:, :, mine] + received_ref[:, :, mine].astype(F32)
            at += half

    dims = (2, rows, sum(halves))
    shapes = [shape(dims, F32), shape(dims, BF16)]
    return small("halve_far", kernel, shapes, bits, *kepts, *receiveds)


def gated(bits, own, received):
    _, rows, width = own.shape

    def kernel(bits_ref, own_ref, received_ref, out_ref):
        gate = own_ref[0] + received_ref[0].astype(F32)
        up = own_ref[1] + received_ref[1].astype(F32)
        out_ref[...] = (gate / (1.0 + jnp.exp(-gate)) * up).astype(BF16)

    return small("gated", kernel, shape((rows, width), BF16), bits, own, received)


def join_far(bits, own, received, halves):
    rows = own.shape[0]

    def kernel(bits_ref, own_ref, received_ref, *out_refs):
        at = 0
        for out_ref, half in zip(out_refs, halves):
            out_ref[:, aligned(bits_ref[FAR], half)] = own_ref[:, at : at + half]
            out_ref[:, aligned(1 - bits_ref[FAR], half)] = received_ref[:, at : at + half]
            at += half

    shapes = [shape((rows, 2 * half), BF16) for half in halves]
    return small("join_far", kernel, shapes, bits, own, received)


def join(bits, bit, own, received):
    rows, half = own.shape

    def kernel(bits_ref, own_ref, received_ref, out_ref):
        out_ref[:, aligned(bits_ref[bit], half)] = own_ref[...]
        out_ref[:, aligned(1 - bits_ref[bit], half)] = received_ref[...]

    return small("join", kernel, shape((rows, 2 * half), BF16), bits, own, received)


def fast_layer(v, gate_weight, up_weight, down_weight):
    gx = lax.axis_index("gx")
    bits = jnp.stack([gx & 1, (gx >> 1) & 1, gx >> 2])
    mine, theirs, at = [], [], 0
    for counts in CHUNKS:
        mine.append([])
        theirs.append([])
        for n, (first, _) in zip(counts, STREAM_BITS):
            mine[-1].append(at + bits[first] * n)
            theirs[-1].append(at + (1 - bits[first]) * n)
            at += 2 * n
    received, kept = [], []
    for c, counts in enumerate(CHUNKS):
        received.append([])
        for n, start, (first, _) in zip(counts, theirs[c], STREAM_BITS):
            (sent,) = gate_up(v, gate_weight, up_weight, [start], [n], BF16)
            received[c].append(swap(sent, first))
        kept.append(gate_up(v, gate_weight, up_weight, mine[c], counts, F32))
    total = None
    for c, counts in enumerate(CHUNKS):
        owns, others = [], []
        for s, (_, second) in enumerate(STREAM_BITS):
            own, send = halve(bits, second, kept[c][s], received[c][s])
            owns.append(own)
            others.append(swap(send, second))
        own, send = halve_far(bits, owns, others)
        hidden = gated(bits, own, swap(send, FAR))
        quarters = join_far(bits, hidden, swap(hidden, FAR), [128 * n for n in counts])
        halves = [
            join(bits, second, q, swap(q, second)) for q, (_, second) in zip(quarters, STREAM_BITS)
        ]
        others = [swap(h, first) for h, (first, _) in zip(halves, STREAM_BITS)]
        total = down(total, halves, down_weight, mine[c])
        total = down(total, others, down_weight, theirs[c])
    return (total + lax.ppermute(total, "gy", [(0, 1), (1, 0)])).astype(BF16)


def fast_body(tokens, gate_weight, up_weight, down_weight):
    own_rows = tokens.shape[1]
    gy = lax.axis_index("gy")
    gate_weight, up_weight, down_weight = (
        pltpu.with_memory_space_constraint(w, pltpu.HBM)
        for w in (gate_weight, up_weight, down_weight)
    )
    rows = lax.all_gather(tokens, "gy", axis=1, tiled=True)
    first_out = fast_layer(rows[0], gate_weight, up_weight, down_weight)
    second_input = (rows[1].astype(F32) + first_out.astype(F32)).astype(BF16)
    second_out = fast_layer(second_input, gate_weight, up_weight, down_weight)
    outs = jnp.stack([first_out, second_out])
    return lax.dynamic_slice_in_dim(outs, gy * own_rows, own_rows, axis=1)


def plain_body(tokens, gate_weight, up_weight, down_weight):
    def layer_apply(local_input):
        row_block = lax.all_gather(local_input, "gy", axis=0, tiled=True)
        batch_rows = row_block.shape[0]
        gate_term = jnp.dot(row_block, gate_weight, preferred_element_type=F32)
        up_term = jnp.dot(row_block, up_weight, preferred_element_type=F32)
        stacked = jnp.concatenate([gate_term, up_term], axis=0)
        summed = lax.psum_scatter(stacked, "gx", scatter_dimension=1, tiled=True)
        hidden_part = (jax.nn.silu(summed[:batch_rows]) * summed[batch_rows:]).astype(BF16)
        partial_out = jnp.dot(
            lax.all_gather(hidden_part, "gx", axis=1, tiled=True),
            down_weight,
            preferred_element_type=F32,
        )
        return lax.psum_scatter(partial_out, "gy", scatter_dimension=0, tiled=True).astype(BF16)

    first_out = layer_apply(tokens[0])
    second_input = (tokens[1].astype(F32) + first_out.astype(F32)).astype(BF16)
    second_out = layer_apply(second_input)
    return jnp.stack([first_out, second_out])


def solution(mesh):
    fast = mesh.shape["gx"] == 8 and mesh.shape["gy"] == 2
    return jax.shard_map(
        fast_body if fast else plain_body,
        mesh=mesh,
        in_specs=(P(None, ("replica", "gy"), "gx"), P("gx", "gy"), P("gx", "gy"), P("gy", "gx")),
        out_specs=P(None, ("replica", "gy"), "gx"),
        check_vma=False,
    )
```

```python
import jax
import jax.numpy as jnp
from jax import lax
from jax.experimental import pallas as pl
from jax.experimental.pallas import tpu as pltpu
from jax.sharding import PartitionSpec as P

BF16 = jnp.bfloat16
F32 = jnp.float32
BLOCK = 512
CHUNKS = ((4, 4), (3, 2))
STREAM_BITS = ((0, 1), (1, 0))
FAR = 2
VMEM = pl.BlockSpec(memory_space=pltpu.VMEM)
ANY = pl.BlockSpec(memory_space=pl.ANY)
HBM = pl.BlockSpec(memory_space=pltpu.HBM)
PARAMS = pltpu.CompilerParams(vmem_limit_bytes=24 * 2**20)


def swap(array, bit):
    return lax.ppermute(array, "gx", [(i, i ^ (1 << bit)) for i in range(8)])


def aligned(index, step):
    return pl.ds(pl.multiple_of(index * step, 128), step)


def device_bit(bit):
    return (lax.axis_index("gx") >> bit) & 1


class Order:
    def __init__(self, first):
        self.last = first

    def call(self, name, kernel, out_shape, in_specs, operands, scratch):
        def ordered(*refs):
            kernel(*refs[: len(operands)], *refs[len(operands) + 1 :])

        out = pl.pallas_call(
            ordered,
            out_shape=out_shape,
            in_specs=in_specs + [ANY],
            out_specs=[VMEM] * len(out_shape),
            scratch_shapes=scratch,
            compiler_params=PARAMS,
            cost_estimate=pl.CostEstimate(flops=0, bytes_accessed=0, transcendentals=0),
            name=name,
        )(*operands, self.last)
        self.last = out[0]
        return list(out)


def shape(dims, dtype):
    return jax.ShapeDtypeStruct(dims, dtype)


def begin_of(rng, i):
    at, n, bit, side = rng
    return at + (device_bit(bit) ^ side) * n + i


def gate_up_copies(gate_ref, up_ref, rng, held_ref, sems):
    def copy(i, which):
        source = (gate_ref, up_ref)[which].at[:, aligned(begin_of(rng, i), BLOCK)]
        return pltpu.make_async_copy(source, held_ref.at[i, which], sems.at[i, which])

    return copy


def down_copies(weight_ref, rng, held_ref, sems):
    def copy(i):
        source = weight_ref.at[aligned(begin_of(rng, i), BLOCK), :]
        return pltpu.make_async_copy(source, held_ref.at[i], sems.at[i])

    return copy


def fetch(order, gate_weight, up_weight, gate_up_ranges, down_weight, down_ranges):
    depth, columns = gate_weight.shape[0], down_weight.shape[1]
    n_gate_up = len(gate_up_ranges)

    def kernel(gate_ref, up_ref, weight_ref, *rest):
        n_out = n_gate_up + len(down_ranges)
        held, sems = rest[:n_out], rest[n_out:]
        copies = []
        for r, rng in enumerate(gate_up_ranges):
            copy = gate_up_copies(gate_ref, up_ref, rng, held[r], sems[r])
            copies += [copy(i, which) for i in range(rng[1]) for which in range(2)]
        for r, rng in enumerate(down_ranges, n_gate_up):
            copy = down_copies(weight_ref, rng, held[r], sems[r])
            copies += [copy(i) for i in range(rng[1])]
        for copy in copies:
            copy.start()
        for copy in copies:
            copy.wait()

    out = order.call(
        "fetch",
        kernel,
        [shape((rng[1], 2, depth, BLOCK), BF16) for rng in gate_up_ranges]
        + [shape((rng[1], BLOCK, columns), BF16) for rng in down_ranges],
        [HBM, HBM, HBM],
        (gate_weight, up_weight, down_weight),
        [pltpu.SemaphoreType.DMA((rng[1], 2)) for rng in gate_up_ranges]
        + [pltpu.SemaphoreType.DMA((rng[1],)) for rng in down_ranges],
    )
    return out[:n_gate_up], out[n_gate_up:]


def gate_up(order, v, gate_weight, up_weight, ranges, out_type, fetched=None):
    rows, depth = v.shape
    counts = [n for _, n, _, _ in ranges]
    blocks = sum(counts)

    def kernel(v_ref, *rest):
        rest = list(rest)
        if fetched is None:
            gate_ref, up_ref = rest[:2]
            out_refs = rest[2 : 2 + len(ranges)]
            scratch_ref, sems = rest[2 + len(ranges) :]
            parts = [pl.ds(sum(counts[:r]), n) for r, n in enumerate(counts)]
            held = [scratch_ref.at[part] for part in parts]
            copies = [
                gate_up_copies(gate_ref, up_ref, rng, h, sems.at[part])
                for rng, h, part in zip(ranges, held, parts)
            ]
            for copy, n in zip(copies, counts):
                for i in range(n):
                    for which in range(2):
                        copy(i, which).start()
        else:
            held, out_refs = rest[: len(ranges)], rest[len(ranges) :]
        for r, n in enumerate(counts):

            @pl.loop(0, n)
            def _(i):
                for which in range(2):
                    if fetched is None:
                        copies[r](i, which).wait()
                    out_refs[r][which, :, aligned(i, BLOCK)] = jnp.dot(
                        v_ref[...], held[r][i, which], preferred_element_type=F32
                    ).astype(out_type)

    if fetched is None:
        operands, specs = (v, gate_weight, up_weight), [VMEM, HBM, HBM]
        scratch = [
            pltpu.VMEM((blocks, 2, depth, BLOCK), BF16),
            pltpu.SemaphoreType.DMA((blocks, 2)),
        ]
    else:
        operands, specs, scratch = (v, *fetched), [VMEM] * (1 + len(fetched)), []
    shapes = [shape((2, rows, n * BLOCK), out_type) for n in counts]
    return order.call("gate_up", kernel, shapes, specs, operands, scratch)


def down(order, total, hiddens, down_weight, ranges, fetched=()):
    rows = hiddens[0].shape[0]
    columns = down_weight.shape[1]
    counts = [n for _, n, _, _ in ranges]
    n_copied = len(ranges) - len(fetched)
    n_held = sum(counts[:n_copied])

    def kernel(*refs):
        refs = list(refs)
        hidden_refs = [refs.pop(0) for _ in ranges]
        total_ref = refs.pop(0) if total is not None else None
        weight_ref = refs.pop(0)
        fetched_refs = [refs.pop(0) for _ in fetched]
        out_ref = refs.pop(0)
        held, copies = [], []
        for r in range(n_copied):
            part = pl.ds(sum(counts[:r]), counts[r])
            held.append(refs[0].at[part])
            copies.append(down_copies(weight_ref, ranges[r], held[r], refs[1].at[part]))
        for copy, n in zip(copies, counts):
            for i in range(n):
                copy(i).start()
        out_ref[...] = jnp.zeros_like(out_ref) if total_ref is None else total_ref[...]
        for r in [*range(n_copied, len(ranges)), *range(n_copied)]:

            @pl.loop(0, counts[r])
            def _(i):
                if r < n_copied:
                    copies[r](i).wait()
                out_ref[...] += jnp.dot(
                    hidden_refs[r][:, aligned(i, BLOCK)],
                    (held + fetched_refs)[r][i],
                    preferred_element_type=F32,
                )

    totals = [] if total is None else [total]
    return order.call(
        "down",
        kernel,
        [shape((rows, columns), F32)],
        [VMEM] * (len(ranges) + len(totals)) + [HBM] + [VMEM] * len(fetched),
        (*hiddens, *totals, down_weight, *fetched),
        [pltpu.VMEM((n_held, BLOCK, columns), BF16), pltpu.SemaphoreType.DMA((n_held,))]
        if n_held
        else [],
    )[0]


def small(order, name, kernel, out_shape, *operands):
    specs = [VMEM] * len(operands)
    return order.call(name, kernel, out_shape, specs, operands, [])


def halve(order, bit, kept, received):
    _, rows, width = kept.shape
    half = width // 2

    def kernel(kept_ref, received_ref, own_ref, send_ref):
        mine, theirs = aligned(device_bit(bit), half), aligned(1 - device_bit(bit), half)
        send_ref[...] = (kept_ref[:, :, theirs] + received_ref[:, :, theirs].astype(F32)).astype(BF16)
        own_ref[...] = kept_ref[:, :, mine] + received_ref[:, :, mine].astype(F32)

    dims = (2, rows, half)
    return small(order, "halve", kernel, [shape(dims, F32), shape(dims, BF16)], kept, received)


def halve_far(order, kepts, receiveds):
    rows = kepts[0].shape[1]
    halves = [k.shape[2] // 2 for k in kepts]

    def kernel(*refs):
        kept_refs, received_refs = refs[: len(halves)], refs[len(halves) : -2]
        own_ref, send_ref = refs[-2:]
        at = 0
        for kept_ref, received_ref, half in zip(kept_refs, received_refs, halves):
            to = slice(at, at + half)
            mine, theirs = aligned(device_bit(FAR), half), aligned(1 - device_bit(FAR), half)
            send_ref[:, :, to] = (
                kept_ref[:, :, theirs] + received_ref[:, :, theirs].astype(F32)
            ).astype(BF16)
            own_ref[:, :, to] = kept_ref[:, :, mine] + received_ref[:, :, mine].astype(F32)
            at += half

    dims = (2, rows, sum(halves))
    shapes = [shape(dims, F32), shape(dims, BF16)]
    return small(order, "halve_far", kernel, shapes, *kepts, *receiveds)


def gated(order, own, received):
    _, rows, width = own.shape

    def kernel(own_ref, received_ref, out_ref):
        gate = own_ref[0] + received_ref[0].astype(F32)
        up = own_ref[1] + received_ref[1].astype(F32)
        out_ref[...] = (gate / (1.0 + jnp.exp(-gate)) * up).astype(BF16)

    return small(order, "gated", kernel, [shape((rows, width), BF16)], own, received)[0]


def join_far(order, own, received, halves):
    rows = own.shape[0]

    def kernel(own_ref, received_ref, *out_refs):
        at = 0
        for out_ref, half in zip(out_refs, halves):
            out_ref[:, aligned(device_bit(FAR), half)] = own_ref[:, at : at + half]
            out_ref[:, aligned(1 - device_bit(FAR), half)] = received_ref[:, at : at + half]
            at += half

    shapes = [shape((rows, 2 * half), BF16) for half in halves]
    return small(order, "join_far", kernel, shapes, own, received)


def join(order, bit, own, received):
    rows, half = own.shape

    def kernel(own_ref, received_ref, out_ref):
        out_ref[:, aligned(device_bit(bit), half)] = own_ref[...]
        out_ref[:, aligned(1 - device_bit(bit), half)] = received_ref[...]

    return small(order, "join", kernel, [shape((rows, 2 * half), BF16)], own, received)[0]


class Chunk:
    def __init__(self, order, at, counts, v, weights):
        self.order, self.counts, self.v, self.weights = order, counts, v, weights
        self.begins = [at + 2 * sum(counts[:s]) for s in range(len(counts))]
        self.received, self.owns, self.others = {}, {}, {}
        self.joined, self.arrived = {}, {}

    def ranges(self, side):
        return [
            (at, n, first, side) for at, n, (first, _) in zip(self.begins, self.counts, STREAM_BITS)
        ]

    def send(self, s, fetched=None):
        held = None if fetched is None else [fetched[s]]
        (sent,) = gate_up(self.order, self.v, *self.weights[:2], [self.ranges(1)[s]], BF16, held)
        self.received[s] = swap(sent, STREAM_BITS[s][0])

    def keep(self):
        self.kept = gate_up(self.order, self.v, *self.weights[:2], self.ranges(0), F32)

    def halve(self, s):
        second = STREAM_BITS[s][1]
        self.owns[s], send = halve(self.order, second, self.kept[s], self.received[s])
        self.others[s] = swap(send, second)

    def halve_far(self):
        self.own, send = halve_far(self.order, [*self.owns.values()], [*self.others.values()])
        self.far = swap(send, FAR)

    def gated(self):
        self.hidden = gated(self.order, self.own, self.far)
        self.far = swap(self.hidden, FAR)

    def join_far(self):
        halves = [128 * n for n in self.counts]
        self.quarters = join_far(self.order, self.hidden, self.far, halves)
        self.others = [swap(q, second) for q, (_, second) in zip(self.quarters, STREAM_BITS)]

    def join(self, s):
        first, second = STREAM_BITS[s]
        self.joined[s] = join(self.order, second, self.quarters[s], self.others[s])
        self.arrived[s] = swap(self.joined[s], first)

    def hiddens(self, side):
        held = self.arrived if side else self.joined
        return [held[s] for s in range(len(self.counts))]


def fast_layer(v, weights, fetched=None, ahead=False):
    order = Order(v)
    a, b = (
        Chunk(order, 2 * sum(map(sum, CHUNKS[:c])), counts, v, weights)
        for c, counts in enumerate(CHUNKS)
    )
    a.send(0, fetched)
    a.send(1, fetched)
    b.send(0)
    b.send(1)
    a.keep()
    a.halve(0)
    a.halve(1)
    b.keep()
    a.halve_far()
    b.halve(0)
    b.halve(1)
    _, b_rows = fetch(order, *weights[:2], [], weights[2], b.ranges(0) + b.ranges(1))
    a.gated()
    b.halve_far()
    next_sends = fetch(order, *weights[:2], a.ranges(1), weights[2], [])[0] if ahead else None
    a.join_far()
    b.gated()
    b.join_far()
    a.join(0)
    a.join(1)
    total = down(order, None, a.hiddens(0), weights[2], a.ranges(0))
    b.join(0)
    b.join(1)
    total = down(order, total, a.hiddens(1), weights[2], a.ranges(1))
    total = down(order, total, b.hiddens(0), weights[2], b.ranges(0), b_rows[:2])
    total = down(order, total, b.hiddens(1), weights[2], b.ranges(1), b_rows[2:])
    return total + lax.ppermute(total, "gy", [(0, 1), (1, 0)]), next_sends


def fast_body(tokens, *weights):
    own_rows = tokens.shape[1]
    gy = lax.axis_index("gy")
    weights = [pltpu.with_memory_space_constraint(w, pltpu.HBM) for w in weights]
    rows = lax.all_gather(tokens, "gy", axis=1, tiled=True)
    first_sum, fetched = fast_layer(rows[0], weights, ahead=True)
    first_out = first_sum.astype(BF16)
    second_input = (rows[1].astype(F32) + first_out.astype(F32)).astype(BF16)
    second_sum, _ = fast_layer(second_input, weights, fetched)
    outs = jnp.stack([first_out, second_sum.astype(BF16)])
    return lax.dynamic_slice_in_dim(outs, gy * own_rows, own_rows, axis=1)


def plain_body(tokens, gate_weight, up_weight, down_weight):
    def layer_apply(local_input):
        row_block = lax.all_gather(local_input, "gy", axis=0, tiled=True)
        batch_rows = row_block.shape[0]
        gate_term = jnp.dot(row_block, gate_weight, preferred_element_type=F32)
        up_term = jnp.dot(row_block, up_weight, preferred_element_type=F32)
        stacked = jnp.concatenate([gate_term, up_term], axis=0)
        summed = lax.psum_scatter(stacked, "gx", scatter_dimension=1, tiled=True)
        hidden_part = (jax.nn.silu(summed[:batch_rows]) * summed[batch_rows:]).astype(BF16)
        partial_out = jnp.dot(
            lax.all_gather(hidden_part, "gx", axis=1, tiled=True),
            down_weight,
            preferred_element_type=F32,
        )
        return lax.psum_scatter(partial_out, "gy", scatter_dimension=0, tiled=True).astype(BF16)

    first_out = layer_apply(tokens[0])
    second_input = (tokens[1].astype(F32) + first_out.astype(F32)).astype(BF16)
    second_out = layer_apply(second_input)
    return jnp.stack([first_out, second_out])


def solution(mesh):
    fast = mesh.shape["gx"] == 8 and mesh.shape["gy"] == 2
    return jax.shard_map(
        fast_body if fast else plain_body,
        mesh=mesh,
        in_specs=(P(None, ("replica", "gy"), "gx"), P("gx", "gy"), P("gx", "gy"), P("gy", "gx")),
        out_specs=P(None, ("replica", "gy"), "gx"),
        check_vma=False,
    )
```

```python
import jax
import jax.numpy as jnp
from jax import lax
from jax.experimental import pallas as pl
from jax.experimental.pallas import tpu as pltpu
from jax.sharding import PartitionSpec as P

BF16 = jnp.bfloat16
F32 = jnp.float32
BLOCK = 512
CHUNKS = ((4, 3), (3, 3))
STREAM_BITS = ((0, 1), (1, 0))
FAR = 2
VMEM = pl.BlockSpec(memory_space=pltpu.VMEM)
ANY = pl.BlockSpec(memory_space=pl.ANY)
HBM = pl.BlockSpec(memory_space=pltpu.HBM)
PARAMS = pltpu.CompilerParams(vmem_limit_bytes=18 * 2**20)


def swap(array, bit):
    return lax.ppermute(array, "gx", [(i, i ^ (1 << bit)) for i in range(8)])


def aligned(index, step):
    return pl.ds(pl.multiple_of(index * step, 128), step)


def device_bit(bit):
    return (lax.axis_index("gx") >> bit) & 1


class Order:
    def __init__(self, first):
        self.last = first

    def call(self, name, kernel, out_shape, in_specs, operands, scratch):
        def ordered(*refs):
            kernel(*refs[: len(operands)], *refs[len(operands) + 1 :])

        out = pl.pallas_call(
            ordered,
            out_shape=out_shape,
            in_specs=in_specs + [ANY],
            out_specs=[VMEM] * len(out_shape),
            scratch_shapes=scratch,
            compiler_params=PARAMS,
            cost_estimate=pl.CostEstimate(flops=0, bytes_accessed=0, transcendentals=0),
            name=name,
        )(*operands, self.last)
        self.last = out[0]
        return list(out)


def shape(dims, dtype):
    return jax.ShapeDtypeStruct(dims, dtype)


def begin_of(rng, i):
    at, n, bit, side = rng
    return at + (device_bit(bit) ^ side) * n + i


def gate_up_copies(gate_ref, up_ref, rng, held_ref, sems):
    def copy(i, which):
        source = (gate_ref, up_ref)[which].at[:, aligned(begin_of(rng, i), BLOCK)]
        return pltpu.make_async_copy(source, held_ref.at[i, which], sems.at[i, which])

    return copy


def down_copies(weight_ref, rng, held_ref, sems):
    def copy(i):
        source = weight_ref.at[aligned(begin_of(rng, i), BLOCK), :]
        return pltpu.make_async_copy(source, held_ref.at[i], sems.at[i])

    return copy


def fetch(order, gate_weight, up_weight, gate_up_ranges, down_weight, down_ranges):
    depth, columns = gate_weight.shape[0], down_weight.shape[1]
    n_gate_up = len(gate_up_ranges)

    def kernel(gate_ref, up_ref, weight_ref, *rest):
        n_out = n_gate_up + len(down_ranges)
        held, sems = rest[:n_out], rest[n_out:]
        copies = []
        for r, rng in enumerate(gate_up_ranges):
            copy = gate_up_copies(gate_ref, up_ref, rng, held[r], sems[r])
            copies += [copy(i, which) for i in range(rng[1]) for which in range(2)]
        for r, rng in enumerate(down_ranges, n_gate_up):
            copy = down_copies(weight_ref, rng, held[r], sems[r])
            copies += [copy(i) for i in range(rng[1])]
        for copy in copies:
            copy.start()
        for copy in copies:
            copy.wait()

    out = order.call(
        "fetch",
        kernel,
        [shape((rng[1], 2, depth, BLOCK), BF16) for rng in gate_up_ranges]
        + [shape((rng[1], BLOCK, columns), BF16) for rng in down_ranges],
        [HBM, HBM, HBM],
        (gate_weight, up_weight, down_weight),
        [pltpu.SemaphoreType.DMA((rng[1], 2)) for rng in gate_up_ranges]
        + [pltpu.SemaphoreType.DMA((rng[1],)) for rng in down_ranges],
    )
    return out[:n_gate_up], out[n_gate_up:]


def gate_up(order, v, gate_weight, up_weight, ranges, out_type, fetched=None):
    rows, depth = v.shape
    counts = [n for _, n, _, _ in ranges]
    blocks = sum(counts)

    def kernel(v_ref, *rest):
        rest = list(rest)
        if fetched is None:
            gate_ref, up_ref = rest[:2]
            out_refs = rest[2 : 2 + len(ranges)]
            scratch_ref, sems = rest[2 + len(ranges) :]
            parts = [pl.ds(sum(counts[:r]), n) for r, n in enumerate(counts)]
            held = [scratch_ref.at[part] for part in parts]
            copies = [
                gate_up_copies(gate_ref, up_ref, rng, h, sems.at[part])
                for rng, h, part in zip(ranges, held, parts)
            ]
            for copy, n in zip(copies, counts):
                for i in range(n):
                    for which in range(2):
                        copy(i, which).start()
        else:
            held, out_refs = rest[: len(ranges)], rest[len(ranges) :]
        for r, n in enumerate(counts):

            @pl.loop(0, n)
            def _(i):
                for which in range(2):
                    if fetched is None:
                        copies[r](i, which).wait()
                    out_refs[r][which, :, aligned(i, BLOCK)] = jnp.dot(
                        v_ref[...], held[r][i, which], preferred_element_type=F32
                    ).astype(out_type)

    if fetched is None:
        operands, specs = (v, gate_weight, up_weight), [VMEM, HBM, HBM]
        scratch = [
            pltpu.VMEM((blocks, 2, depth, BLOCK), BF16),
            pltpu.SemaphoreType.DMA((blocks, 2)),
        ]
    else:
        operands, specs, scratch = (v, *fetched), [VMEM] * (1 + len(fetched)), []
    shapes = [shape((2, rows, n * BLOCK), out_type) for n in counts]
    return order.call("gate_up", kernel, shapes, specs, operands, scratch)


def down(order, total, hiddens, down_weight, ranges, fetched=()):
    rows = hiddens[0].shape[0]
    columns = down_weight.shape[1]
    counts = [n for _, n, _, _ in ranges]
    n_copied = len(ranges) - len(fetched)
    n_held = sum(counts[:n_copied])

    def kernel(*refs):
        refs = list(refs)
        hidden_refs = [refs.pop(0) for _ in ranges]
        total_ref = refs.pop(0) if total is not None else None
        weight_ref = refs.pop(0)
        fetched_refs = [refs.pop(0) for _ in fetched]
        out_ref = refs.pop(0)
        held, copies = [], []
        for r in range(n_copied):
            part = pl.ds(sum(counts[:r]), counts[r])
            held.append(refs[0].at[part])
            copies.append(down_copies(weight_ref, ranges[r], held[r], refs[1].at[part]))
        for copy, n in zip(copies, counts):
            for i in range(n):
                copy(i).start()
        out_ref[...] = jnp.zeros_like(out_ref) if total_ref is None else total_ref[...]
        for r in [*range(n_copied, len(ranges)), *range(n_copied)]:

            @pl.loop(0, counts[r])
            def _(i):
                if r < n_copied:
                    copies[r](i).wait()
                out_ref[...] += jnp.dot(
                    hidden_refs[r][:, aligned(i, BLOCK)],
                    (held + fetched_refs)[r][i],
                    preferred_element_type=F32,
                )

    totals = [] if total is None else [total]
    return order.call(
        "down",
        kernel,
        [shape((rows, columns), F32)],
        [VMEM] * (len(ranges) + len(totals)) + [HBM] + [VMEM] * len(fetched),
        (*hiddens, *totals, down_weight, *fetched),
        [pltpu.VMEM((n_held, BLOCK, columns), BF16), pltpu.SemaphoreType.DMA((n_held,))]
        if n_held
        else [],
    )[0]


def small(order, name, kernel, out_shape, *operands):
    specs = [VMEM] * len(operands)
    return order.call(name, kernel, out_shape, specs, operands, [])


def halve(order, bit, kept, received):
    _, rows, width = kept.shape
    half = width // 2

    def kernel(kept_ref, received_ref, own_ref, send_ref):
        mine, theirs = aligned(device_bit(bit), half), aligned(1 - device_bit(bit), half)
        send_ref[...] = (kept_ref[:, :, theirs] + received_ref[:, :, theirs].astype(F32)).astype(BF16)
        own_ref[...] = kept_ref[:, :, mine] + received_ref[:, :, mine].astype(F32)

    dims = (2, rows, half)
    return small(order, "halve", kernel, [shape(dims, F32), shape(dims, BF16)], kept, received)


def halve_far(order, kepts, receiveds):
    rows = kepts[0].shape[1]
    halves = [k.shape[2] // 2 for k in kepts]

    def kernel(*refs):
        kept_refs, received_refs = refs[: len(halves)], refs[len(halves) : -2]
        own_ref, send_ref = refs[-2:]
        at = 0
        for kept_ref, received_ref, half in zip(kept_refs, received_refs, halves):
            to = slice(at, at + half)
            mine, theirs = aligned(device_bit(FAR), half), aligned(1 - device_bit(FAR), half)
            send_ref[:, :, to] = (
                kept_ref[:, :, theirs] + received_ref[:, :, theirs].astype(F32)
            ).astype(BF16)
            own_ref[:, :, to] = kept_ref[:, :, mine] + received_ref[:, :, mine].astype(F32)
            at += half

    dims = (2, rows, sum(halves))
    shapes = [shape(dims, F32), shape(dims, BF16)]
    return small(order, "halve_far", kernel, shapes, *kepts, *receiveds)


def gated(order, own, received):
    _, rows, width = own.shape

    def kernel(own_ref, received_ref, out_ref):
        gate = own_ref[0] + received_ref[0].astype(F32)
        up = own_ref[1] + received_ref[1].astype(F32)
        out_ref[...] = (gate / (1.0 + jnp.exp(-gate)) * up).astype(BF16)

    return small(order, "gated", kernel, [shape((rows, width), BF16)], own, received)[0]


def join_far(order, own, received, halves):
    rows = own.shape[0]

    def kernel(own_ref, received_ref, *out_refs):
        at = 0
        for out_ref, half in zip(out_refs, halves):
            out_ref[:, aligned(device_bit(FAR), half)] = own_ref[:, at : at + half]
            out_ref[:, aligned(1 - device_bit(FAR), half)] = received_ref[:, at : at + half]
            at += half

    shapes = [shape((rows, 2 * half), BF16) for half in halves]
    return small(order, "join_far", kernel, shapes, own, received)


def join(order, bit, own, received):
    rows, half = own.shape

    def kernel(own_ref, received_ref, out_ref):
        out_ref[:, aligned(device_bit(bit), half)] = own_ref[...]
        out_ref[:, aligned(1 - device_bit(bit), half)] = received_ref[...]

    return small(order, "join", kernel, [shape((rows, 2 * half), BF16)], own, received)[0]


class Chunk:
    def __init__(self, order, at, counts, v, weights):
        self.order, self.counts, self.v, self.weights = order, counts, v, weights
        self.begins = [at + 2 * sum(counts[:s]) for s in range(len(counts))]
        self.received, self.owns, self.others = {}, {}, {}
        self.joined, self.arrived = {}, {}

    def ranges(self, side):
        return [
            (at, n, first, side) for at, n, (first, _) in zip(self.begins, self.counts, STREAM_BITS)
        ]

    def send(self, s, fetched=None):
        held = None if fetched is None else [fetched[s]]
        (sent,) = gate_up(self.order, self.v, *self.weights[:2], [self.ranges(1)[s]], BF16, held)
        self.received[s] = swap(sent, STREAM_BITS[s][0])

    def keep(self):
        self.kept = gate_up(self.order, self.v, *self.weights[:2], self.ranges(0), F32)

    def halve(self, s):
        second = STREAM_BITS[s][1]
        self.owns[s], send = halve(self.order, second, self.kept[s], self.received[s])
        self.others[s] = swap(send, second)

    def halve_far(self):
        self.own, send = halve_far(self.order, [*self.owns.values()], [*self.others.values()])
        self.far = swap(send, FAR)

    def gated(self):
        self.hidden = gated(self.order, self.own, self.far)
        self.far = swap(self.hidden, FAR)

    def join_far(self):
        halves = [128 * n for n in self.counts]
        self.quarters = join_far(self.order, self.hidden, self.far, halves)
        self.others = [swap(q, second) for q, (_, second) in zip(self.quarters, STREAM_BITS)]

    def join(self, s):
        first, second = STREAM_BITS[s]
        self.joined[s] = join(self.order, second, self.quarters[s], self.others[s])
        self.arrived[s] = swap(self.joined[s], first)

    def hiddens(self, side):
        held = self.arrived if side else self.joined
        return [held[s] for s in range(len(self.counts))]


def fast_layer(v, weights, fetched=None, ahead=False):
    order = Order(v)
    a, b = (
        Chunk(order, 2 * sum(map(sum, CHUNKS[:c])), counts, v, weights)
        for c, counts in enumerate(CHUNKS)
    )
    a.send(0, fetched)
    a.send(1, fetched)
    b.send(0, fetched and fetched[2:])
    b.send(1, fetched and fetched[2:])
    a.keep()
    a.halve(0)
    a.halve(1)
    b.keep()
    b.halve(0)
    b.halve(1)
    a.halve_far()
    _, ab_rows = fetch(order, *weights[:2], [], weights[2], a.ranges(1) + b.ranges(1))
    b.halve_far()
    next_sends = fetch(order, *weights[:2], b.ranges(1), weights[2], [])[0] if ahead else None
    a.gated()
    next_sends = fetch(order, *weights[:2], a.ranges(1), weights[2], [])[0] + next_sends if ahead else None
    b.gated()
    a.join_far()
    b.join_far()
    a.join(0)
    a.join(1)
    b.join(0)
    b.join(1)
    total = down(order, None, a.hiddens(0) + b.hiddens(0), weights[2], a.ranges(0) + b.ranges(0))
    total = down(order, total, a.hiddens(1), weights[2], a.ranges(1), ab_rows[:2])
    total = down(order, total, b.hiddens(1), weights[2], b.ranges(1), ab_rows[2:])
    return total + lax.ppermute(total, "gy", [(0, 1), (1, 0)]), next_sends


def pair_rows(own, gy):
    other = lax.ppermute(own, "gy", [(0, 1), (1, 0)])
    return jnp.where(gy == 0, jnp.concatenate([own, other]), jnp.concatenate([other, own]))


def fast_body(tokens, *weights):
    own_rows = tokens.shape[1]
    gy = lax.axis_index("gy")
    weights = [pltpu.with_memory_space_constraint(w, pltpu.HBM) for w in weights]
    rows = [pair_rows(t, gy) for t in tokens]
    first_sum, fetched = fast_layer(rows[0], weights, ahead=True)
    first_out = first_sum.astype(BF16)
    second_input = (rows[1].astype(F32) + first_out.astype(F32)).astype(BF16)
    second_sum, _ = fast_layer(second_input, weights, fetched)
    outs = jnp.stack([first_out, second_sum.astype(BF16)])
    return lax.dynamic_slice_in_dim(outs, gy * own_rows, own_rows, axis=1)


def plain_body(tokens, gate_weight, up_weight, down_weight):
    def layer_apply(local_input):
        row_block = lax.all_gather(local_input, "gy", axis=0, tiled=True)
        batch_rows = row_block.shape[0]
        gate_term = jnp.dot(row_block, gate_weight, preferred_element_type=F32)
        up_term = jnp.dot(row_block, up_weight, preferred_element_type=F32)
        stacked = jnp.concatenate([gate_term, up_term], axis=0)
        summed = lax.psum_scatter(stacked, "gx", scatter_dimension=1, tiled=True)
        hidden_part = (jax.nn.silu(summed[:batch_rows]) * summed[batch_rows:]).astype(BF16)
        partial_out = jnp.dot(
            lax.all_gather(hidden_part, "gx", axis=1, tiled=True),
            down_weight,
            preferred_element_type=F32,
        )
        return lax.psum_scatter(partial_out, "gy", scatter_dimension=0, tiled=True).astype(BF16)

    first_out = layer_apply(tokens[0])
    second_input = (tokens[1].astype(F32) + first_out.astype(F32)).astype(BF16)
    second_out = layer_apply(second_input)
    return jnp.stack([first_out, second_out])


def solution(mesh):
    fast = mesh.shape["gx"] == 8 and mesh.shape["gy"] == 2
    return jax.shard_map(
        fast_body if fast else plain_body,
        mesh=mesh,
        in_specs=(P(None, ("replica", "gy"), "gx"), P("gx", "gy"), P("gx", "gy"), P("gy", "gx")),
        out_specs=P(None, ("replica", "gy"), "gx"),
        check_vma=False,
    )
```

```python
import jax
import jax.numpy as jnp
from jax import lax
from jax.experimental import pallas as pl
from jax.experimental.pallas import tpu as pltpu
from jax.sharding import PartitionSpec as P

BF16 = jnp.bfloat16
F32 = jnp.float32
BLOCK = 512
CHUNKS = ((4, 3), (3, 3))
STREAM_BITS = ((0, 1), (1, 0))
FAR = 2
VMEM = pl.BlockSpec(memory_space=pltpu.VMEM)
ANY = pl.BlockSpec(memory_space=pl.ANY)
HBM = pl.BlockSpec(memory_space=pltpu.HBM)
PARAMS = pltpu.CompilerParams(vmem_limit_bytes=18 * 2**20)


def swap(array, bit):
    return lax.ppermute(array, "gx", [(i, i ^ (1 << bit)) for i in range(8)])


def aligned(index, step):
    return pl.ds(pl.multiple_of(index * step, 128), step)


def device_bit(bit):
    return (lax.axis_index("gx") >> bit) & 1


class Order:
    def __init__(self, first):
        self.last = first

    def call(self, name, kernel, out_shape, in_specs, operands, scratch):
        def ordered(*refs):
            kernel(*refs[: len(operands)], *refs[len(operands) + 1 :])

        out = pl.pallas_call(
            ordered,
            out_shape=out_shape,
            in_specs=in_specs + [ANY],
            out_specs=[VMEM] * len(out_shape),
            scratch_shapes=scratch,
            compiler_params=PARAMS,
            cost_estimate=pl.CostEstimate(flops=0, bytes_accessed=0, transcendentals=0),
            name=name,
        )(*operands, self.last)
        self.last = out[0]
        return list(out)


def shape(dims, dtype):
    return jax.ShapeDtypeStruct(dims, dtype)


def begin_of(rng, i):
    at, n, bit, side = rng
    return at + (device_bit(bit) ^ side) * n + i


def gate_up_copies(gate_ref, up_ref, rng, held_ref, sems):
    def copy(i, which):
        source = (gate_ref, up_ref)[which].at[:, aligned(begin_of(rng, i), BLOCK)]
        return pltpu.make_async_copy(source, held_ref.at[i, which], sems.at[i, which])

    return copy


def down_copies(weight_ref, rng, held_ref, sems):
    def copy(i):
        source = weight_ref.at[aligned(begin_of(rng, i), BLOCK), :]
        return pltpu.make_async_copy(source, held_ref.at[i], sems.at[i])

    return copy


def fetch(order, gate_weight, up_weight, gate_up_ranges, down_weight, down_ranges):
    depth, columns = gate_weight.shape[0], down_weight.shape[1]
    n_gate_up = len(gate_up_ranges)

    def kernel(gate_ref, up_ref, weight_ref, *rest):
        n_out = n_gate_up + len(down_ranges)
        held, sems = rest[:n_out], rest[n_out:]
        copies = []
        for r, rng in enumerate(gate_up_ranges):
            copy = gate_up_copies(gate_ref, up_ref, rng, held[r], sems[r])
            copies += [copy(i, which) for i in range(rng[1]) for which in range(2)]
        for r, rng in enumerate(down_ranges, n_gate_up):
            copy = down_copies(weight_ref, rng, held[r], sems[r])
            copies += [copy(i) for i in range(rng[1])]
        for copy in copies:
            copy.start()
        for copy in copies:
            copy.wait()

    out = order.call(
        "fetch",
        kernel,
        [shape((rng[1], 2, depth, BLOCK), BF16) for rng in gate_up_ranges]
        + [shape((rng[1], BLOCK, columns), BF16) for rng in down_ranges],
        [HBM, HBM, HBM],
        (gate_weight, up_weight, down_weight),
        [pltpu.SemaphoreType.DMA((rng[1], 2)) for rng in gate_up_ranges]
        + [pltpu.SemaphoreType.DMA((rng[1],)) for rng in down_ranges],
    )
    return out[:n_gate_up], out[n_gate_up:]


def gate_up(order, v, gate_weight, up_weight, ranges, out_type, fetched=None):
    rows, depth = v.shape
    counts = [n for _, n, _, _ in ranges]
    blocks = sum(counts)

    def kernel(v_ref, *rest):
        rest = list(rest)
        if fetched is None:
            gate_ref, up_ref = rest[:2]
            out_refs = rest[2 : 2 + len(ranges)]
            scratch_ref, sems = rest[2 + len(ranges) :]
            parts = [pl.ds(sum(counts[:r]), n) for r, n in enumerate(counts)]
            held = [scratch_ref.at[part] for part in parts]
            copies = [
                gate_up_copies(gate_ref, up_ref, rng, h, sems.at[part])
                for rng, h, part in zip(ranges, held, parts)
            ]
            for copy, n in zip(copies, counts):
                for i in range(n):
                    for which in range(2):
                        copy(i, which).start()
        else:
            held, out_refs = rest[: len(ranges)], rest[len(ranges) :]
        for r, n in enumerate(counts):

            @pl.loop(0, n)
            def _(i):
                for which in range(2):
                    if fetched is None:
                        copies[r](i, which).wait()
                    out_refs[r][which, :, aligned(i, BLOCK)] = jnp.dot(
                        v_ref[...], held[r][i, which], preferred_element_type=F32
                    ).astype(out_type)

    if fetched is None:
        operands, specs = (v, gate_weight, up_weight), [VMEM, HBM, HBM]
        scratch = [
            pltpu.VMEM((blocks, 2, depth, BLOCK), BF16),
            pltpu.SemaphoreType.DMA((blocks, 2)),
        ]
    else:
        operands, specs, scratch = (v, *fetched), [VMEM] * (1 + len(fetched)), []
    shapes = [shape((2, rows, n * BLOCK), out_type) for n in counts]
    return order.call("gate_up", kernel, shapes, specs, operands, scratch)


def down(order, total, hiddens, down_weight, ranges, fetched=()):
    rows = hiddens[0].shape[0]
    columns = down_weight.shape[1]
    counts = [n for _, n, _, _ in ranges]
    n_copied = len(ranges) - len(fetched)
    n_held = sum(counts[:n_copied])

    def kernel(*refs):
        refs = list(refs)
        hidden_refs = [refs.pop(0) for _ in ranges]
        total_ref = refs.pop(0) if total is not None else None
        weight_ref = refs.pop(0)
        fetched_refs = [refs.pop(0) for _ in fetched]
        out_ref = refs.pop(0)
        held, copies = [], []
        for r in range(n_copied):
            part = pl.ds(sum(counts[:r]), counts[r])
            held.append(refs[0].at[part])
            copies.append(down_copies(weight_ref, ranges[r], held[r], refs[1].at[part]))
        for copy, n in zip(copies, counts):
            for i in range(n):
                copy(i).start()
        out_ref[...] = jnp.zeros_like(out_ref) if total_ref is None else total_ref[...]
        for r in [*range(n_copied, len(ranges)), *range(n_copied)]:

            @pl.loop(0, counts[r])
            def _(i):
                if r < n_copied:
                    copies[r](i).wait()
                out_ref[...] += jnp.dot(
                    hidden_refs[r][:, aligned(i, BLOCK)],
                    (held + fetched_refs)[r][i],
                    preferred_element_type=F32,
                )

    totals = [] if total is None else [total]
    return order.call(
        "down",
        kernel,
        [shape((rows, columns), F32)],
        [VMEM] * (len(ranges) + len(totals)) + [HBM] + [VMEM] * len(fetched),
        (*hiddens, *totals, down_weight, *fetched),
        [pltpu.VMEM((n_held, BLOCK, columns), BF16), pltpu.SemaphoreType.DMA((n_held,))]
        if n_held
        else [],
    )[0]


def small(order, name, kernel, out_shape, *operands):
    specs = [VMEM] * len(operands)
    return order.call(name, kernel, out_shape, specs, operands, [])


def halve(order, bit, kept, received):
    _, rows, width = kept.shape
    half = width // 2

    def kernel(kept_ref, received_ref, own_ref, send_ref):
        mine, theirs = aligned(device_bit(bit), half), aligned(1 - device_bit(bit), half)
        send_ref[...] = (kept_ref[:, :, theirs] + received_ref[:, :, theirs].astype(F32)).astype(BF16)
        own_ref[...] = kept_ref[:, :, mine] + received_ref[:, :, mine].astype(F32)

    dims = (2, rows, half)
    return small(order, "halve", kernel, [shape(dims, F32), shape(dims, BF16)], kept, received)


def halve_far(order, kepts, receiveds):
    rows = kepts[0].shape[1]
    halves = [k.shape[2] // 2 for k in kepts]

    def kernel(*refs):
        kept_refs, received_refs = refs[: len(halves)], refs[len(halves) : -2]
        own_ref, send_ref = refs[-2:]
        at = 0
        for kept_ref, received_ref, half in zip(kept_refs, received_refs, halves):
            to = slice(at, at + half)
            mine, theirs = aligned(device_bit(FAR), half), aligned(1 - device_bit(FAR), half)
            send_ref[:, :, to] = (
                kept_ref[:, :, theirs] + received_ref[:, :, theirs].astype(F32)
            ).astype(BF16)
            own_ref[:, :, to] = kept_ref[:, :, mine] + received_ref[:, :, mine].astype(F32)
            at += half

    dims = (2, rows, sum(halves))
    shapes = [shape(dims, F32), shape(dims, BF16)]
    return small(order, "halve_far", kernel, shapes, *kepts, *receiveds)


def gated(order, own, received):
    _, rows, width = own.shape

    def kernel(own_ref, received_ref, out_ref):
        gate = own_ref[0] + received_ref[0].astype(F32)
        up = own_ref[1] + received_ref[1].astype(F32)
        out_ref[...] = (gate / (1.0 + jnp.exp(-gate)) * up).astype(BF16)

    return small(order, "gated", kernel, [shape((rows, width), BF16)], own, received)[0]


def join_far(order, own, received, halves):
    rows = own.shape[0]

    def kernel(own_ref, received_ref, *out_refs):
        at = 0
        for out_ref, half in zip(out_refs, halves):
            out_ref[:, aligned(device_bit(FAR), half)] = own_ref[:, at : at + half]
            out_ref[:, aligned(1 - device_bit(FAR), half)] = received_ref[:, at : at + half]
            at += half

    shapes = [shape((rows, 2 * half), BF16) for half in halves]
    return small(order, "join_far", kernel, shapes, own, received)


def join(order, bit, own, received):
    rows, half = own.shape

    def kernel(own_ref, received_ref, out_ref):
        out_ref[:, aligned(device_bit(bit), half)] = own_ref[...]
        out_ref[:, aligned(1 - device_bit(bit), half)] = received_ref[...]

    return small(order, "join", kernel, [shape((rows, 2 * half), BF16)], own, received)[0]


class Chunk:
    def __init__(self, order, at, counts, v, weights):
        self.order, self.counts, self.v, self.weights = order, counts, v, weights
        self.begins = [at + 2 * sum(counts[:s]) for s in range(len(counts))]
        self.received, self.owns, self.others = {}, {}, {}
        self.joined, self.arrived = {}, {}

    def ranges(self, side):
        return [
            (at, n, first, side) for at, n, (first, _) in zip(self.begins, self.counts, STREAM_BITS)
        ]

    def send(self, s, fetched=None):
        held = None if fetched is None else [fetched[s]]
        (sent,) = gate_up(self.order, self.v, *self.weights[:2], [self.ranges(1)[s]], BF16, held)
        self.received[s] = swap(sent, STREAM_BITS[s][0])

    def keep(self):
        self.kept = gate_up(self.order, self.v, *self.weights[:2], self.ranges(0), F32)

    def halve(self, s):
        second = STREAM_BITS[s][1]
        self.owns[s], send = halve(self.order, second, self.kept[s], self.received[s])
        self.others[s] = swap(send, second)

    def halve_far(self):
        self.own, send = halve_far(self.order, [*self.owns.values()], [*self.others.values()])
        self.far = swap(send, FAR)

    def gated(self):
        self.hidden = gated(self.order, self.own, self.far)
        self.far = swap(self.hidden, FAR)

    def join_far(self):
        halves = [128 * n for n in self.counts]
        self.quarters = join_far(self.order, self.hidden, self.far, halves)
        self.others = [swap(q, second) for q, (_, second) in zip(self.quarters, STREAM_BITS)]

    def join(self, s):
        first, second = STREAM_BITS[s]
        self.joined[s] = join(self.order, second, self.quarters[s], self.others[s])
        self.arrived[s] = swap(self.joined[s], first)

    def hiddens(self, side):
        held = self.arrived if side else self.joined
        return [held[s] for s in range(len(self.counts))]


def fast_layer(v, weights, fetched=None, ahead=False):
    order = Order(v)
    a, b = (
        Chunk(order, 2 * sum(map(sum, CHUNKS[:c])), counts, v, weights)
        for c, counts in enumerate(CHUNKS)
    )
    a.send(0, fetched)
    a.send(1, fetched)
    b.send(0, fetched and fetched[2:])
    b.send(1, fetched and fetched[2:])
    a.keep()
    a.halve(0)
    a.halve(1)
    b.keep()
    b.halve(0)
    b.halve(1)
    a.halve_far()
    _, ab_rows = fetch(order, *weights[:2], [], weights[2], a.ranges(1) + b.ranges(1))
    b.halve_far()
    if ahead:
        next_sends, own_rows = fetch(order, *weights[:2], b.ranges(1), weights[2], [])[0], ()
    else:
        next_sends = None
        own_rows = fetch(order, *weights[:2], [], weights[2], a.ranges(0) + b.ranges(0))[1]
    a.gated()
    if ahead:
        next_sends = fetch(order, *weights[:2], a.ranges(1), weights[2], [])[0] + next_sends
    b.gated()
    a.join_far()
    b.join_far()
    a.join(0)
    a.join(1)
    b.join(0)
    b.join(1)
    total = down(order, None, a.hiddens(0) + b.hiddens(0), weights[2], a.ranges(0) + b.ranges(0), own_rows)
    total = down(order, total, a.hiddens(1), weights[2], a.ranges(1), ab_rows[:2])
    total = down(order, total, b.hiddens(1), weights[2], b.ranges(1), ab_rows[2:])
    return total + lax.ppermute(total, "gy", [(0, 1), (1, 0)]), next_sends


def pair_rows(own, gy):
    other = lax.ppermute(own, "gy", [(0, 1), (1, 0)])
    return jnp.where(gy == 0, jnp.concatenate([own, other]), jnp.concatenate([other, own]))


def fast_body(tokens, *weights):
    own_rows = tokens.shape[1]
    gy = lax.axis_index("gy")
    weights = [pltpu.with_memory_space_constraint(w, pltpu.HBM) for w in weights]
    rows = [pair_rows(t, gy) for t in tokens]
    first_sum, fetched = fast_layer(rows[0], weights, ahead=True)
    first_out = first_sum.astype(BF16)
    second_input = (rows[1].astype(F32) + first_out.astype(F32)).astype(BF16)
    second_sum, _ = fast_layer(second_input, weights, fetched)
    outs = jnp.stack([first_out, second_sum.astype(BF16)])
    return lax.dynamic_slice_in_dim(outs, gy * own_rows, own_rows, axis=1)


def plain_body(tokens, gate_weight, up_weight, down_weight):
    def layer_apply(local_input):
        row_block = lax.all_gather(local_input, "gy", axis=0, tiled=True)
        batch_rows = row_block.shape[0]
        gate_term = jnp.dot(row_block, gate_weight, preferred_element_type=F32)
        up_term = jnp.dot(row_block, up_weight, preferred_element_type=F32)
        stacked = jnp.concatenate([gate_term, up_term], axis=0)
        summed = lax.psum_scatter(stacked, "gx", scatter_dimension=1, tiled=True)
        hidden_part = (jax.nn.silu(summed[:batch_rows]) * summed[batch_rows:]).astype(BF16)
        partial_out = jnp.dot(
            lax.all_gather(hidden_part, "gx", axis=1, tiled=True),
            down_weight,
            preferred_element_type=F32,
        )
        return lax.psum_scatter(partial_out, "gy", scatter_dimension=0, tiled=True).astype(BF16)

    first_out = layer_apply(tokens[0])
    second_input = (tokens[1].astype(F32) + first_out.astype(F32)).astype(BF16)
    second_out = layer_apply(second_input)
    return jnp.stack([first_out, second_out])


def solution(mesh):
    fast = mesh.shape["gx"] == 8 and mesh.shape["gy"] == 2
    return jax.shard_map(
        fast_body if fast else plain_body,
        mesh=mesh,
        in_specs=(P(None, ("replica", "gy"), "gx"), P("gx", "gy"), P("gx", "gy"), P("gy", "gx")),
        out_specs=P(None, ("replica", "gy"), "gx"),
        check_vma=False,
    )
```

```python
import jax
import jax.numpy as jnp
from jax import lax
from jax.experimental import pallas as pl
from jax.experimental.pallas import tpu as pltpu
from jax.sharding import PartitionSpec as P

BF16 = jnp.bfloat16
F32 = jnp.float32
BLOCK = 512
CHUNKS = ((4, 3), (3, 3))
STREAM_BITS = ((0, 1), (1, 0))
FAR = 2
VMEM = pl.BlockSpec(memory_space=pltpu.VMEM)
ANY = pl.BlockSpec(memory_space=pl.ANY)
HBM = pl.BlockSpec(memory_space=pltpu.HBM)
PARAMS = pltpu.CompilerParams(vmem_limit_bytes=16 * 2**20)


def swap(array, bit):
    return lax.ppermute(array, "gx", [(i, i ^ (1 << bit)) for i in range(8)])


def aligned(index, step):
    return pl.ds(pl.multiple_of(index * step, 128), step)


def device_bit(bit):
    return (lax.axis_index("gx") >> bit) & 1


class Order:
    def __init__(self, first):
        self.last = first

    def call(self, name, kernel, out_shape, in_specs, operands, scratch):
        def ordered(*refs):
            kernel(*refs[: len(operands)], *refs[len(operands) + 1 :])

        out = pl.pallas_call(
            ordered,
            out_shape=out_shape,
            in_specs=in_specs + [ANY],
            out_specs=[VMEM] * len(out_shape),
            scratch_shapes=scratch,
            compiler_params=PARAMS,
            cost_estimate=pl.CostEstimate(flops=0, bytes_accessed=0, transcendentals=0),
            name=name,
        )(*operands, self.last)
        self.last = out[0]
        return list(out)


def shape(dims, dtype):
    return jax.ShapeDtypeStruct(dims, dtype)


def begin_of(rng, i):
    at, n, bit, side = rng
    return at + (device_bit(bit) ^ side) * n + i


def gate_up_copies(gate_ref, up_ref, rng, held_ref, sems):
    def copy(i, which):
        source = (gate_ref, up_ref)[which].at[:, aligned(begin_of(rng, i), BLOCK)]
        return pltpu.make_async_copy(source, held_ref.at[i, which], sems.at[i, which])

    return copy


def down_copies(weight_ref, rng, held_ref, sems):
    def copy(i):
        source = weight_ref.at[aligned(begin_of(rng, i), BLOCK), :]
        return pltpu.make_async_copy(source, held_ref.at[i], sems.at[i])

    return copy


def fetch(order, gate_weight, up_weight, gate_up_ranges, down_weight, down_ranges):
    depth, columns = gate_weight.shape[0], down_weight.shape[1]
    n_gate_up = len(gate_up_ranges)

    def kernel(gate_ref, up_ref, weight_ref, *rest):
        n_out = n_gate_up + len(down_ranges)
        held, sems = rest[:n_out], rest[n_out:]
        copies = []
        for r, rng in enumerate(gate_up_ranges):
            copy = gate_up_copies(gate_ref, up_ref, rng, held[r], sems[r])
            copies += [copy(i, which) for i in range(rng[1]) for which in range(2)]
        for r, rng in enumerate(down_ranges, n_gate_up):
            copy = down_copies(weight_ref, rng, held[r], sems[r])
            copies += [copy(i) for i in range(rng[1])]
        for copy in copies:
            copy.start()
        for copy in copies:
            copy.wait()

    out = order.call(
        "fetch",
        kernel,
        [shape((rng[1], 2, depth, BLOCK), BF16) for rng in gate_up_ranges]
        + [shape((rng[1], BLOCK, columns), BF16) for rng in down_ranges],
        [HBM, HBM, HBM],
        (gate_weight, up_weight, down_weight),
        [pltpu.SemaphoreType.DMA((rng[1], 2)) for rng in gate_up_ranges]
        + [pltpu.SemaphoreType.DMA((rng[1],)) for rng in down_ranges],
    )
    return out[:n_gate_up], out[n_gate_up:]


def gate_up(order, v, gate_weight, up_weight, ranges, out_type, fetched=None):
    rows, depth = v.shape
    counts = [n for _, n, _, _ in ranges]
    blocks = sum(counts)

    def kernel(v_ref, *rest):
        rest = list(rest)
        if fetched is None:
            gate_ref, up_ref = rest[:2]
            out_refs = rest[2 : 2 + len(ranges)]
            scratch_ref, sems = rest[2 + len(ranges) :]
            parts = [pl.ds(sum(counts[:r]), n) for r, n in enumerate(counts)]
            held = [scratch_ref.at[part] for part in parts]
            copies = [
                gate_up_copies(gate_ref, up_ref, rng, h, sems.at[part])
                for rng, h, part in zip(ranges, held, parts)
            ]
            for copy, n in zip(copies, counts):
                for i in range(n):
                    for which in range(2):
                        copy(i, which).start()
        else:
            held, out_refs = rest[: len(ranges)], rest[len(ranges) :]
        for r, n in enumerate(counts):

            @pl.loop(0, n)
            def _(i):
                for which in range(2):
                    if fetched is None:
                        copies[r](i, which).wait()
                    out_refs[r][which, :, aligned(i, BLOCK)] = jnp.dot(
                        v_ref[...], held[r][i, which], preferred_element_type=F32
                    ).astype(out_type)

    if fetched is None:
        operands, specs = (v, gate_weight, up_weight), [VMEM, HBM, HBM]
        scratch = [
            pltpu.VMEM((blocks, 2, depth, BLOCK), BF16),
            pltpu.SemaphoreType.DMA((blocks, 2)),
        ]
    else:
        operands, specs, scratch = (v, *fetched), [VMEM] * (1 + len(fetched)), []
    shapes = [shape((2, rows, n * BLOCK), out_type) for n in counts]
    return order.call("gate_up", kernel, shapes, specs, operands, scratch)


def down(order, total, hiddens, down_weight, ranges, fetched=()):
    rows = hiddens[0].shape[0]
    columns = down_weight.shape[1]
    counts = [n for _, n, _, _ in ranges]
    n_copied = len(ranges) - len(fetched)
    n_held = sum(counts[:n_copied])

    def kernel(*refs):
        refs = list(refs)
        hidden_refs = [refs.pop(0) for _ in ranges]
        total_ref = refs.pop(0) if total is not None else None
        weight_ref = refs.pop(0)
        fetched_refs = [refs.pop(0) for _ in fetched]
        out_ref = refs.pop(0)
        held, copies = [], []
        for r in range(n_copied):
            part = pl.ds(sum(counts[:r]), counts[r])
            held.append(refs[0].at[part])
            copies.append(down_copies(weight_ref, ranges[r], held[r], refs[1].at[part]))
        for copy, n in zip(copies, counts):
            for i in range(n):
                copy(i).start()
        out_ref[...] = jnp.zeros_like(out_ref) if total_ref is None else total_ref[...]
        for r in [*range(n_copied, len(ranges)), *range(n_copied)]:

            @pl.loop(0, counts[r])
            def _(i):
                if r < n_copied:
                    copies[r](i).wait()
                out_ref[...] += jnp.dot(
                    hidden_refs[r][:, aligned(i, BLOCK)],
                    (held + fetched_refs)[r][i],
                    preferred_element_type=F32,
                )

    totals = [] if total is None else [total]
    return order.call(
        "down",
        kernel,
        [shape((rows, columns), F32)],
        [VMEM] * (len(ranges) + len(totals)) + [HBM] + [VMEM] * len(fetched),
        (*hiddens, *totals, down_weight, *fetched),
        [pltpu.VMEM((n_held, BLOCK, columns), BF16), pltpu.SemaphoreType.DMA((n_held,))]
        if n_held
        else [],
    )[0]


def small(order, name, kernel, out_shape, *operands):
    specs = [VMEM] * len(operands)
    return order.call(name, kernel, out_shape, specs, operands, [])


def halve(order, bit, kept, received):
    _, rows, width = kept.shape
    half = width // 2

    def kernel(kept_ref, received_ref, own_ref, send_ref):
        mine, theirs = aligned(device_bit(bit), half), aligned(1 - device_bit(bit), half)
        send_ref[...] = (kept_ref[:, :, theirs] + received_ref[:, :, theirs].astype(F32)).astype(BF16)
        own_ref[...] = kept_ref[:, :, mine] + received_ref[:, :, mine].astype(F32)

    dims = (2, rows, half)
    return small(order, "halve", kernel, [shape(dims, F32), shape(dims, BF16)], kept, received)


def halve_far(order, kepts, receiveds):
    rows = kepts[0].shape[1]
    halves = [k.shape[2] // 2 for k in kepts]

    def kernel(*refs):
        kept_refs, received_refs = refs[: len(halves)], refs[len(halves) : -2]
        own_ref, send_ref = refs[-2:]
        at = 0
        for kept_ref, received_ref, half in zip(kept_refs, received_refs, halves):
            to = slice(at, at + half)
            mine, theirs = aligned(device_bit(FAR), half), aligned(1 - device_bit(FAR), half)
            send_ref[:, :, to] = (
                kept_ref[:, :, theirs] + received_ref[:, :, theirs].astype(F32)
            ).astype(BF16)
            own_ref[:, :, to] = kept_ref[:, :, mine] + received_ref[:, :, mine].astype(F32)
            at += half

    dims = (2, rows, sum(halves))
    shapes = [shape(dims, F32), shape(dims, BF16)]
    return small(order, "halve_far", kernel, shapes, *kepts, *receiveds)


def gated(order, own, received):
    _, rows, width = own.shape

    def kernel(own_ref, received_ref, out_ref):
        gate = own_ref[0] + received_ref[0].astype(F32)
        up = own_ref[1] + received_ref[1].astype(F32)
        out_ref[...] = (gate / (1.0 + jnp.exp(-gate)) * up).astype(BF16)

    return small(order, "gated", kernel, [shape((rows, width), BF16)], own, received)[0]


def join_far(order, own, received, halves):
    rows = own.shape[0]

    def kernel(own_ref, received_ref, *out_refs):
        at = 0
        for out_ref, half in zip(out_refs, halves):
            out_ref[:, aligned(device_bit(FAR), half)] = own_ref[:, at : at + half]
            out_ref[:, aligned(1 - device_bit(FAR), half)] = received_ref[:, at : at + half]
            at += half

    shapes = [shape((rows, 2 * half), BF16) for half in halves]
    return small(order, "join_far", kernel, shapes, own, received)


def join(order, bit, own, received):
    rows, half = own.shape

    def kernel(own_ref, received_ref, out_ref):
        out_ref[:, aligned(device_bit(bit), half)] = own_ref[...]
        out_ref[:, aligned(1 - device_bit(bit), half)] = received_ref[...]

    return small(order, "join", kernel, [shape((rows, 2 * half), BF16)], own, received)[0]


class Chunk:
    def __init__(self, order, at, counts, v, weights):
        self.order, self.counts, self.v, self.weights = order, counts, v, weights
        self.begins = [at + 2 * sum(counts[:s]) for s in range(len(counts))]
        self.received, self.owns, self.others = {}, {}, {}
        self.joined, self.arrived = {}, {}

    def ranges(self, side):
        return [
            (at, n, first, side) for at, n, (first, _) in zip(self.begins, self.counts, STREAM_BITS)
        ]

    def send(self, s, fetched=None):
        held = None if fetched is None else [fetched[s]]
        (sent,) = gate_up(self.order, self.v, *self.weights[:2], [self.ranges(1)[s]], BF16, held)
        self.received[s] = swap(sent, STREAM_BITS[s][0])

    def keep(self):
        self.kept = gate_up(self.order, self.v, *self.weights[:2], self.ranges(0), F32)

    def halve(self, s):
        second = STREAM_BITS[s][1]
        self.owns[s], send = halve(self.order, second, self.kept[s], self.received[s])
        self.others[s] = swap(send, second)

    def halve_far(self):
        self.own, send = halve_far(self.order, [*self.owns.values()], [*self.others.values()])
        self.far = swap(send, FAR)

    def gated(self):
        self.hidden = gated(self.order, self.own, self.far)
        self.far = swap(self.hidden, FAR)

    def join_far(self):
        halves = [128 * n for n in self.counts]
        self.quarters = join_far(self.order, self.hidden, self.far, halves)
        self.others = [swap(q, second) for q, (_, second) in zip(self.quarters, STREAM_BITS)]

    def join(self, s):
        first, second = STREAM_BITS[s]
        self.joined[s] = join(self.order, second, self.quarters[s], self.others[s])
        self.arrived[s] = swap(self.joined[s], first)

    def hiddens(self, side):
        held = self.arrived if side else self.joined
        return [held[s] for s in range(len(self.counts))]


def fast_layer(v, weights, fetched=None, ahead=False):
    order = Order(v)
    a, b = (
        Chunk(order, 2 * sum(map(sum, CHUNKS[:c])), counts, v, weights)
        for c, counts in enumerate(CHUNKS)
    )
    a.send(0, fetched)
    a.send(1, fetched)
    b.send(0, fetched and fetched[2:])
    b.send(1, fetched and fetched[2:])
    a.keep()
    a.halve(0)
    a.halve(1)
    b.keep()
    b.halve(0)
    b.halve(1)
    a.halve_far()
    _, ab_rows = fetch(order, *weights[:2], [], weights[2], a.ranges(1) + b.ranges(1))
    b.halve_far()
    if ahead:
        next_sends, own_rows = fetch(order, *weights[:2], b.ranges(1), weights[2], [])[0], ()
    else:
        next_sends = None
        own_rows = fetch(order, *weights[:2], [], weights[2], a.ranges(0) + b.ranges(0))[1]
    a.gated()
    if ahead:
        next_sends = fetch(order, *weights[:2], a.ranges(1), weights[2], [])[0] + next_sends
    b.gated()
    a.join_far()
    b.join_far()
    a.join(0)
    a.join(1)
    b.join(0)
    b.join(1)
    total = down(order, None, a.hiddens(0) + b.hiddens(0), weights[2], a.ranges(0) + b.ranges(0), own_rows)
    total = down(order, total, a.hiddens(1), weights[2], a.ranges(1), ab_rows[:2])
    total = down(order, total, b.hiddens(1), weights[2], b.ranges(1), ab_rows[2:])
    return total + lax.ppermute(total, "gy", [(0, 1), (1, 0)]), next_sends


def pair_rows(own, gy):
    other = lax.ppermute(own, "gy", [(0, 1), (1, 0)])
    return jnp.where(gy == 0, jnp.concatenate([own, other]), jnp.concatenate([other, own]))


def fast_body(tokens, *weights):
    own_rows = tokens.shape[1]
    gy = lax.axis_index("gy")
    weights = [pltpu.with_memory_space_constraint(w, pltpu.HBM) for w in weights]
    rows = [pair_rows(t, gy) for t in tokens]
    first_sum, fetched = fast_layer(rows[0], weights, ahead=True)
    first_out = first_sum.astype(BF16)
    second_input = (rows[1].astype(F32) + first_out.astype(F32)).astype(BF16)
    second_sum, _ = fast_layer(second_input, weights, fetched)
    outs = jnp.stack([first_out, second_sum.astype(BF16)])
    return lax.dynamic_slice_in_dim(outs, gy * own_rows, own_rows, axis=1)


def plain_body(tokens, gate_weight, up_weight, down_weight):
    def layer_apply(local_input):
        row_block = lax.all_gather(local_input, "gy", axis=0, tiled=True)
        batch_rows = row_block.shape[0]
        gate_term = jnp.dot(row_block, gate_weight, preferred_element_type=F32)
        up_term = jnp.dot(row_block, up_weight, preferred_element_type=F32)
        stacked = jnp.concatenate([gate_term, up_term], axis=0)
        summed = lax.psum_scatter(stacked, "gx", scatter_dimension=1, tiled=True)
        hidden_part = (jax.nn.silu(summed[:batch_rows]) * summed[batch_rows:]).astype(BF16)
        partial_out = jnp.dot(
            lax.all_gather(hidden_part, "gx", axis=1, tiled=True),
            down_weight,
            preferred_element_type=F32,
        )
        return lax.psum_scatter(partial_out, "gy", scatter_dimension=0, tiled=True).astype(BF16)

    first_out = layer_apply(tokens[0])
    second_input = (tokens[1].astype(F32) + first_out.astype(F32)).astype(BF16)
    second_out = layer_apply(second_input)
    return jnp.stack([first_out, second_out])


def solution(mesh):
    fast = mesh.shape["gx"] == 8 and mesh.shape["gy"] == 2
    return jax.shard_map(
        fast_body if fast else plain_body,
        mesh=mesh,
        in_specs=(P(None, ("replica", "gy"), "gx"), P("gx", "gy"), P("gx", "gy"), P("gy", "gx")),
        out_specs=P(None, ("replica", "gy"), "gx"),
        check_vma=False,
    )
```

```python
import jax
import jax.numpy as jnp
from jax import lax
from jax.experimental import pallas as pl
from jax.experimental.pallas import tpu as pltpu
from jax.sharding import PartitionSpec as P

BF16 = jnp.bfloat16
F32 = jnp.float32
BLOCK = 512
CHUNKS = ((4, 3), (3, 3))
STREAM_BITS = ((0, 1), (1, 0))
FAR = 2
VMEM = pl.BlockSpec(memory_space=pltpu.VMEM)
ANY = pl.BlockSpec(memory_space=pl.ANY)
HBM = pl.BlockSpec(memory_space=pltpu.HBM)
PARAMS = pltpu.CompilerParams(vmem_limit_bytes=16 * 2**20)


def swap(array, bit):
    return lax.ppermute(array, "gx", [(i, i ^ (1 << bit)) for i in range(8)])


def aligned(index, step):
    return pl.ds(pl.multiple_of(index * step, 128), step)


def device_bit(bit):
    return (lax.axis_index("gx") >> bit) & 1


class Order:
    def __init__(self, first):
        self.last = first

    def call(self, name, kernel, out_shape, in_specs, operands, scratch):
        def ordered(*refs):
            kernel(*refs[: len(operands)], *refs[len(operands) + 1 :])

        out = pl.pallas_call(
            ordered,
            out_shape=out_shape,
            in_specs=in_specs + [ANY],
            out_specs=[VMEM] * len(out_shape),
            scratch_shapes=scratch,
            compiler_params=PARAMS,
            cost_estimate=pl.CostEstimate(flops=0, bytes_accessed=0, transcendentals=0),
            name=name,
        )(*operands, self.last)
        self.last = out[0]
        return list(out)


def shape(dims, dtype):
    return jax.ShapeDtypeStruct(dims, dtype)


def begin_of(rng, i):
    at, n, bit, side = rng
    return at + (device_bit(bit) ^ side) * n + i


def gate_up_copies(gate_ref, up_ref, rng, held_ref, sems):
    def copy(i, which):
        source = (gate_ref, up_ref)[which].at[:, aligned(begin_of(rng, i), BLOCK)]
        return pltpu.make_async_copy(source, held_ref.at[i, which], sems.at[i, which])

    return copy


def down_copies(weight_ref, rng, held_ref, sems):
    def copy(i):
        source = weight_ref.at[aligned(begin_of(rng, i), BLOCK), :]
        return pltpu.make_async_copy(source, held_ref.at[i], sems.at[i])

    return copy


def fetch(order, gate_weight, up_weight, gate_up_ranges, down_weight, down_ranges):
    depth, columns = gate_weight.shape[0], down_weight.shape[1]
    n_gate_up = len(gate_up_ranges)

    def kernel(gate_ref, up_ref, weight_ref, *rest):
        n_out = n_gate_up + len(down_ranges)
        held, sems = rest[:n_out], rest[n_out:]
        copies = []
        for r, rng in enumerate(gate_up_ranges):
            copy = gate_up_copies(gate_ref, up_ref, rng, held[r], sems[r])
            copies += [copy(i, which) for i in range(rng[1]) for which in range(2)]
        for r, rng in enumerate(down_ranges, n_gate_up):
            copy = down_copies(weight_ref, rng, held[r], sems[r])
            copies += [copy(i) for i in range(rng[1])]
        for copy in copies:
            copy.start()
        for copy in copies:
            copy.wait()

    out = order.call(
        "fetch",
        kernel,
        [shape((rng[1], 2, depth, BLOCK), BF16) for rng in gate_up_ranges]
        + [shape((rng[1], BLOCK, columns), BF16) for rng in down_ranges],
        [HBM, HBM, HBM],
        (gate_weight, up_weight, down_weight),
        [pltpu.SemaphoreType.DMA((rng[1], 2)) for rng in gate_up_ranges]
        + [pltpu.SemaphoreType.DMA((rng[1],)) for rng in down_ranges],
    )
    return out[:n_gate_up], out[n_gate_up:]


def gate_up(order, v, gate_weight, up_weight, ranges, out_type, fetched=None):
    rows, depth = v.shape
    counts = [n for _, n, _, _ in ranges]
    blocks = sum(counts)

    def kernel(v_ref, *rest):
        rest = list(rest)
        if fetched is None:
            gate_ref, up_ref = rest[:2]
            out_refs = rest[2 : 2 + len(ranges)]
            scratch_ref, sems = rest[2 + len(ranges) :]
            parts = [pl.ds(sum(counts[:r]), n) for r, n in enumerate(counts)]
            held = [scratch_ref.at[part] for part in parts]
            copies = [
                gate_up_copies(gate_ref, up_ref, rng, h, sems.at[part])
                for rng, h, part in zip(ranges, held, parts)
            ]
            for copy, n in zip(copies, counts):
                for i in range(n):
                    for which in range(2):
                        copy(i, which).start()
        else:
            held, out_refs = rest[: len(ranges)], rest[len(ranges) :]
        for r, n in enumerate(counts):

            @pl.loop(0, n)
            def _(i):
                for which in range(2):
                    if fetched is None:
                        copies[r](i, which).wait()
                    out_refs[r][which, :, aligned(i, BLOCK)] = jnp.dot(
                        v_ref[...], held[r][i, which], preferred_element_type=F32
                    ).astype(out_type)

    if fetched is None:
        operands, specs = (v, gate_weight, up_weight), [VMEM, HBM, HBM]
        scratch = [
            pltpu.VMEM((blocks, 2, depth, BLOCK), BF16),
            pltpu.SemaphoreType.DMA((blocks, 2)),
        ]
    else:
        operands, specs, scratch = (v, *fetched), [VMEM] * (1 + len(fetched)), []
    shapes = [shape((2, rows, n * BLOCK), out_type) for n in counts]
    return order.call("gate_up", kernel, shapes, specs, operands, scratch)


def down(order, total, hiddens, down_weight, ranges, fetched=()):
    rows = hiddens[0].shape[0]
    columns = down_weight.shape[1]
    counts = [n for _, n, _, _ in ranges]
    n_copied = len(ranges) - len(fetched)
    n_held = sum(counts[:n_copied])

    def kernel(*refs):
        refs = list(refs)
        hidden_refs = [refs.pop(0) for _ in ranges]
        total_ref = refs.pop(0) if total is not None else None
        weight_ref = refs.pop(0)
        fetched_refs = [refs.pop(0) for _ in fetched]
        out_ref = refs.pop(0)
        held, copies = [], []
        for r in range(n_copied):
            part = pl.ds(sum(counts[:r]), counts[r])
            held.append(refs[0].at[part])
            copies.append(down_copies(weight_ref, ranges[r], held[r], refs[1].at[part]))
        for copy, n in zip(copies, counts):
            for i in range(n):
                copy(i).start()
        out_ref[...] = jnp.zeros_like(out_ref) if total_ref is None else total_ref[...]
        for r in [*range(n_copied, len(ranges)), *range(n_copied)]:

            @pl.loop(0, counts[r])
            def _(i):
                if r < n_copied:
                    copies[r](i).wait()
                out_ref[...] += jnp.dot(
                    hidden_refs[r][:, aligned(i, BLOCK)],
                    (held + fetched_refs)[r][i],
                    preferred_element_type=F32,
                )

    totals = [] if total is None else [total]
    return order.call(
        "down",
        kernel,
        [shape((rows, columns), F32)],
        [VMEM] * (len(ranges) + len(totals)) + [HBM] + [VMEM] * len(fetched),
        (*hiddens, *totals, down_weight, *fetched),
        [pltpu.VMEM((n_held, BLOCK, columns), BF16), pltpu.SemaphoreType.DMA((n_held,))]
        if n_held
        else [],
    )[0]


def small(order, name, kernel, out_shape, *operands):
    specs = [VMEM] * len(operands)
    return order.call(name, kernel, out_shape, specs, operands, [])


def halve(order, bit, kept, received):
    _, rows, width = kept.shape
    half = width // 2

    def kernel(kept_ref, received_ref, own_ref, send_ref):
        mine, theirs = aligned(device_bit(bit), half), aligned(1 - device_bit(bit), half)
        send_ref[...] = (kept_ref[:, :, theirs] + received_ref[:, :, theirs].astype(F32)).astype(BF16)
        own_ref[...] = kept_ref[:, :, mine] + received_ref[:, :, mine].astype(F32)

    dims = (2, rows, half)
    return small(order, "halve", kernel, [shape(dims, F32), shape(dims, BF16)], kept, received)


def halve_far(order, kepts, receiveds):
    rows = kepts[0].shape[1]
    halves = [k.shape[2] // 2 for k in kepts]

    def kernel(*refs):
        kept_refs, received_refs = refs[: len(halves)], refs[len(halves) : -2]
        own_ref, send_ref = refs[-2:]
        at = 0
        for kept_ref, received_ref, half in zip(kept_refs, received_refs, halves):
            to = slice(at, at + half)
            mine, theirs = aligned(device_bit(FAR), half), aligned(1 - device_bit(FAR), half)
            send_ref[:, :, to] = (
                kept_ref[:, :, theirs] + received_ref[:, :, theirs].astype(F32)
            ).astype(BF16)
            own_ref[:, :, to] = kept_ref[:, :, mine] + received_ref[:, :, mine].astype(F32)
            at += half

    dims = (2, rows, sum(halves))
    shapes = [shape(dims, F32), shape(dims, BF16)]
    return small(order, "halve_far", kernel, shapes, *kepts, *receiveds)


def gated(order, own, received):
    _, rows, width = own.shape

    def kernel(own_ref, received_ref, out_ref):
        gate = own_ref[0] + received_ref[0].astype(F32)
        up = own_ref[1] + received_ref[1].astype(F32)
        out_ref[...] = (gate / (1.0 + jnp.exp(-gate)) * up).astype(BF16)

    return small(order, "gated", kernel, [shape((rows, width), BF16)], own, received)[0]


def join_far(order, own, received, halves):
    rows = own.shape[0]

    def kernel(own_ref, received_ref, *out_refs):
        at = 0
        for out_ref, half in zip(out_refs, halves):
            out_ref[:, aligned(device_bit(FAR), half)] = own_ref[:, at : at + half]
            out_ref[:, aligned(1 - device_bit(FAR), half)] = received_ref[:, at : at + half]
            at += half

    shapes = [shape((rows, 2 * half), BF16) for half in halves]
    return small(order, "join_far", kernel, shapes, own, received)


def join(order, bit, own, received):
    rows, half = own.shape

    def kernel(own_ref, received_ref, out_ref):
        out_ref[:, aligned(device_bit(bit), half)] = own_ref[...]
        out_ref[:, aligned(1 - device_bit(bit), half)] = received_ref[...]

    return small(order, "join", kernel, [shape((rows, 2 * half), BF16)], own, received)[0]


class Chunk:
    def __init__(self, order, at, counts, v, weights):
        self.order, self.counts, self.v, self.weights = order, counts, v, weights
        self.begins = [at + 2 * sum(counts[:s]) for s in range(len(counts))]
        self.received, self.owns, self.others = {}, {}, {}
        self.joined, self.arrived = {}, {}

    def ranges(self, side):
        return [
            (at, n, first, side) for at, n, (first, _) in zip(self.begins, self.counts, STREAM_BITS)
        ]

    def send(self, s, fetched=None):
        held = None if fetched is None else [fetched[s]]
        (sent,) = gate_up(self.order, self.v, *self.weights[:2], [self.ranges(1)[s]], BF16, held)
        self.received[s] = swap(sent, STREAM_BITS[s][0])

    def keep(self):
        self.kept = gate_up(self.order, self.v, *self.weights[:2], self.ranges(0), F32)

    def halve(self, s):
        second = STREAM_BITS[s][1]
        self.owns[s], send = halve(self.order, second, self.kept[s], self.received[s])
        self.others[s] = swap(send, second)

    def halve_far(self):
        self.own, send = halve_far(self.order, [*self.owns.values()], [*self.others.values()])
        self.far = swap(send, FAR)

    def gated(self):
        self.hidden = gated(self.order, self.own, self.far)
        self.far = swap(self.hidden, FAR)

    def join_far(self):
        halves = [128 * n for n in self.counts]
        self.quarters = join_far(self.order, self.hidden, self.far, halves)
        self.others = [swap(q, second) for q, (_, second) in zip(self.quarters, STREAM_BITS)]

    def join(self, s):
        first, second = STREAM_BITS[s]
        self.joined[s] = join(self.order, second, self.quarters[s], self.others[s])
        self.arrived[s] = swap(self.joined[s], first)

    def hiddens(self, side):
        held = self.arrived if side else self.joined
        return [held[s] for s in range(len(self.counts))]


def fast_layer(v, weights, fetched=None, ahead=False):
    order = Order(v)
    a, b = (
        Chunk(order, 2 * sum(map(sum, CHUNKS[:c])), counts, v, weights)
        for c, counts in enumerate(CHUNKS)
    )
    a.send(0, fetched)
    a.send(1, fetched)
    b.send(0, fetched and fetched[2:])
    b.send(1, fetched and fetched[2:])
    a.keep()
    a.halve(0)
    a.halve(1)
    b.keep()
    b.halve(0)
    b.halve(1)
    a.halve_far()
    _, ab_rows = fetch(order, *weights[:2], [], weights[2], a.ranges(1) + b.ranges(1))
    b.halve_far()
    if ahead:
        next_sends, own_rows = fetch(order, *weights[:2], b.ranges(1), weights[2], [])[0], ()
    else:
        next_sends = None
        own_rows = fetch(order, *weights[:2], [], weights[2], a.ranges(0) + b.ranges(0))[1]
    a.gated()
    if ahead:
        next_sends = fetch(order, *weights[:2], a.ranges(1), weights[2], [])[0] + next_sends
    b.gated()
    a.join_far()
    b.join_far()
    a.join(0)
    a.join(1)
    b.join(0)
    b.join(1)
    total = down(order, None, a.hiddens(0) + b.hiddens(0), weights[2], a.ranges(0) + b.ranges(0), own_rows)
    total = down(order, total, a.hiddens(1), weights[2], a.ranges(1), ab_rows[:2])
    total = down(order, total, b.hiddens(1), weights[2], b.ranges(1), ab_rows[2:])
    return total, next_sends


def pair_rows(own, gy):
    other = lax.ppermute(own, "gy", [(0, 1), (1, 0)])
    return jnp.where(gy == 0, jnp.concatenate([own, other]), jnp.concatenate([other, own]))


def fast_body(tokens, *weights):
    own_rows = tokens.shape[1]
    gy = lax.axis_index("gy")
    weights = [pltpu.with_memory_space_constraint(w, pltpu.HBM) for w in weights]
    rows = [pair_rows(t, gy) for t in tokens]
    total, fetched = fast_layer(rows[0], weights, ahead=True)
    first_out = (total + lax.ppermute(total, "gy", [(0, 1), (1, 0)])).astype(BF16)
    second_input = (rows[1].astype(F32) + first_out.astype(F32)).astype(BF16)
    total, _ = fast_layer(second_input, weights, fetched)
    first_out = jnp.where(gy == 0, first_out[:own_rows], first_out[own_rows:])
    own = jnp.where(gy == 0, total[:own_rows], total[own_rows:])
    other = jnp.where(gy == 0, total[own_rows:], total[:own_rows])
    second_out = (own + lax.ppermute(other, "gy", [(0, 1), (1, 0)])).astype(BF16)
    return jnp.stack([first_out, second_out])


def plain_body(tokens, gate_weight, up_weight, down_weight):
    def layer_apply(local_input):
        row_block = lax.all_gather(local_input, "gy", axis=0, tiled=True)
        batch_rows = row_block.shape[0]
        gate_term = jnp.dot(row_block, gate_weight, preferred_element_type=F32)
        up_term = jnp.dot(row_block, up_weight, preferred_element_type=F32)
        stacked = jnp.concatenate([gate_term, up_term], axis=0)
        summed = lax.psum_scatter(stacked, "gx", scatter_dimension=1, tiled=True)
        hidden_part = (jax.nn.silu(summed[:batch_rows]) * summed[batch_rows:]).astype(BF16)
        partial_out = jnp.dot(
            lax.all_gather(hidden_part, "gx", axis=1, tiled=True),
            down_weight,
            preferred_element_type=F32,
        )
        return lax.psum_scatter(partial_out, "gy", scatter_dimension=0, tiled=True).astype(BF16)

    first_out = layer_apply(tokens[0])
    second_input = (tokens[1].astype(F32) + first_out.astype(F32)).astype(BF16)
    second_out = layer_apply(second_input)
    return jnp.stack([first_out, second_out])


def solution(mesh):
    fast = mesh.shape["gx"] == 8 and mesh.shape["gy"] == 2
    return jax.shard_map(
        fast_body if fast else plain_body,
        mesh=mesh,
        in_specs=(P(None, ("replica", "gy"), "gx"), P("gx", "gy"), P("gx", "gy"), P("gy", "gx")),
        out_specs=P(None, ("replica", "gy"), "gx"),
        check_vma=False,
    )
```
